32 devices in a mesh: groups: 2 (over x), seq: 16 (over z, y, core).
Axes of the slice: x: 2, y: 2, z: 4, core: 2. Of those that a mesh axis runs over, the one named last changes fastest.
Arguments:
- delta_query: bfloat16 [4096, 8, 128], P(('groups', 'seq')), parts along dimension 0, may hold values from -6 to 6
- delta_key: bfloat16 [4096, 8, 128], P(('groups', 'seq')), parts along dimension 0, may hold values from -6 to 6
- delta_value: bfloat16 [4096, 16, 128], P(('groups', 'seq')), parts along dimension 0, may hold values from -6 to 6
- log_decay: float32 [4096, 16], P(('groups', 'seq')), parts along dimension 0, may hold values from -0.8 to 0
- write_logit: float32 [4096, 16], P(('groups', 'seq')), parts along dimension 0, may hold values from -8 to 6
- output_gate: bfloat16 [4096, 16, 128], P(('groups', 'seq')), parts along dimension 0, may hold values from -6 to 6
- attn_query: bfloat16 [4096, 8, 256], P(('groups', 'seq')), parts along dimension 0, may hold values from -96 to 96
- attn_key: bfloat16 [4096, 2, 256], P(('groups', 'seq')), parts along dimension 0, may hold values from -5 to 5
- attn_value: bfloat16 [4096, 2, 256], P(('groups', 'seq')), parts along dimension 0, may hold values from -6 to 6
- attn_gate: bfloat16 [4096, 8, 256], P(('groups', 'seq')), parts along dimension 0, may hold values from -6 to 6
- doc_ids: int32 [64], P('groups'), parts along dimension 0, may hold values from 0 to 7, never falling along the last dimension, each value on 1 to 8 neighbouring positions
Outputs:
- delta_out: bfloat16 [4096, 16, 128], P(('groups', 'seq')), parts along dimension 0
- attn_out: bfloat16 [4096, 8, 256], P(('groups', 'seq')), parts along dimension 0
The draws below stay inside these ranges and needn't reach their ends.
There are 2 independent parts, one for each index of `groups`. The reference program is written for one: setup_inputs(seed, part) draws one part's arguments, and reference() takes and returns one part's arrays. A program takes and returns all parts, laid end to end along the dimension named above; each array names one. Nothing has to cross between parts.
Inputs may be any that keep to these rules, and one draw needn't show every extreme that they name: `doc_ids`: never falls from block to block; each document covers 1 to 8 blocks, and one covers exactly 8.
All inputs are finite; a program needn't handle non-finite values.
Results may differ from the reference program's by a relative error of at most 0.0055.
Values may be sent and summed in bfloat16 or wider, within the bound.
A program may use at most 320 MiB of HBM per device.

```python
import math
import jax
import jax.numpy as jnp
import numpy as np
from jax import lax

HD = 128
VALUE_HEADS = 16
KH = 8
QH = 8
KVH = 2
AD = 256
BLK = 64
SPAN = 4
TOK_DEV = 128
CONTEXT_TOKENS = 2048
NBLK = 32
DOC_BLK = 8
DOCS = 8


def draw_log_decay(key, part):
    random_subkeys = jax.random.split(jax.random.fold_in(key, 5), 6)
    extent_span = SPAN * TOK_DEV
    forgetful = jax.random.uniform(random_subkeys[0], (VALUE_HEADS,)) < 0.5
    slow_rate = jnp.exp(jax.random.uniform(random_subkeys[1], (VALUE_HEADS,), minval=math.log(0.1 / extent_span), maxval=math.log(0.5 / extent_span)))
    fast_rate = jnp.exp(jax.random.uniform(random_subkeys[2], (VALUE_HEADS,), minval=math.log(1.0 / 50.0), maxval=math.log(1.0 / 30.0)))
    baseline_rate = jnp.where(forgetful, fast_rate, slow_rate)
    random_noise = jax.random.uniform(random_subkeys[3], (CONTEXT_TOKENS, VALUE_HEADS), minval=0.5, maxval=2.0)
    surges = jax.random.uniform(random_subkeys[4], (CONTEXT_TOKENS, VALUE_HEADS)) < 2.0 / extent_span
    surge_loss = jnp.log(jax.random.uniform(random_subkeys[5], (CONTEXT_TOKENS, VALUE_HEADS), minval=0.5, maxval=0.8))
    return (-baseline_rate[None, :] * random_noise + jnp.where(surges, surge_loss, 0.0)).astype(jnp.float32)


def draw_write_logit(key, part):
    random_subkeys = jax.random.split(jax.random.fold_in(key, 7), 4)
    extent_span = SPAN * TOK_DEV
    order = jax.random.permutation(random_subkeys[0], VALUE_HEADS)
    weak_count = VALUE_HEADS // 2
    strong = jnp.clip(1.5 * jax.random.normal(random_subkeys[1], (CONTEXT_TOKENS, VALUE_HEADS)), -6.0, 6.0)
    weak = order < weak_count
    head_level = jnp.exp(jax.random.uniform(random_subkeys[2], (VALUE_HEADS,), minval=math.log(0.2 * HD / extent_span), maxval=math.log(0.5 * HD / extent_span)))
    random_noise = jnp.exp(jax.random.uniform(random_subkeys[3], (CONTEXT_TOKENS, VALUE_HEADS), minval=math.log(0.5), maxval=math.log(2.0)))
    small = head_level[None, :] * random_noise
    weak_logit = jnp.log(small) - jnp.log1p(-small)
    return jnp.clip(jnp.where(weak[None, :], weak_logit, strong), -8.0, 6.0).astype(jnp.float32)


def attention_pair(key):
    random_subkeys = jax.random.split(jax.random.fold_in(key, 11), 2)
    key_rows = jnp.clip(jax.random.normal(random_subkeys[0], (CONTEXT_TOKENS, KVH, AD)), -4.0, 4.0)
    query_rows = jnp.clip(jax.random.normal(random_subkeys[1], (CONTEXT_TOKENS, QH, AD)), -4.0, 4.0)
    return (query_rows, key_rows)


def draw_attn_query(key, part):
    return attention_pair(key)[0].astype(jnp.bfloat16)


def draw_attn_key(key, part):
    return attention_pair(key)[1].astype(jnp.bfloat16)


def block_levels(stream_key, dims, cuts, smallest, largest):
    level, own = 1.0, jax.random.fold_in(stream_key, 6)
    for position, shards_of in cuts:
        heights = jnp.exp(jax.random.uniform(jax.random.fold_in(own, position), (shards_of,), jnp.float32, smallest / len(cuts), largest / len(cuts)))
        level = level * jnp.repeat(heights, dims[position] // shards_of).reshape([-1 if axis == position else 1 for axis in range(len(dims))])
    return level


def profile(amount, total, most, skew):
    weights = [(1 << 20) // math.isqrt(rank ** skew) + 1 for rank in range(2, amount + 1)]
    rest, counts = total - most - (amount - 1), [1] * (amount - 1)
    while rest > 0:
        candidates = [i for i in range(amount - 1) if counts[i] < most]
        whole, left = sum([weights[i] for i in candidates]), rest
        for i in candidates:
            addition = min(most - counts[i], max(1, left * weights[i] // whole), rest)
            counts[i] = counts[i] + addition
            rest = rest - addition
    return np.array([most] + counts)


def uneven_parts(rng, count, total, bound, lean):
    if count == 2:
        one = jax.random.randint(rng, (), max(1, total - bound), min(bound, total - 1) + 1)
        return jnp.stack([one, total - one])
    sizes = jnp.asarray(profile(count, total, bound, lean), jnp.int32)
    pairs = (count - 1) // 2
    donor, taker = sizes[1:1 + 2 * pairs:2], sizes[2:2 + 2 * pairs:2]
    margin = jnp.minimum(donor - 1, bound - taker)
    passed = jax.random.randint(jax.random.fold_in(rng, 1), (pairs,), 0, 1 << 20) % (margin + 1)
    sizes = sizes.at[1:1 + 2 * pairs:2].set(donor - passed).at[2:2 + 2 * pairs:2].set(taker + passed)
    return sizes[jax.random.permutation(jax.random.fold_in(rng, 2), count)]


def normal_values(key, extent, scale, bound, pieces=(), held_as=jnp.bfloat16):
    values = scale * jax.random.normal(key, extent, jnp.float32)
    if pieces:
        values = values * block_levels(key, extent, pieces, -0.22, 0.18)
    return jnp.clip(values, -bound, bound).astype(held_as)


def setup_inputs(seed: int = 0, part: int = 0) -> dict:
    keys = jax.random.split(jax.random.key(seed), 12)
    part_splits = jax.random.split(jax.random.fold_in(keys[11], part), 12)
    delta_query = normal_values(part_splits[0], (CONTEXT_TOKENS, KH, HD), 1.0, 6.0, ((0, 16),))
    delta_key = normal_values(part_splits[1], (CONTEXT_TOKENS, KH, HD), 1.0, 6.0, ((0, 16),))
    delta_value = normal_values(part_splits[2], (CONTEXT_TOKENS, VALUE_HEADS, HD), 1.0, 6.0, ((0, 16),))
    log_decay = draw_log_decay(jax.random.fold_in(jax.random.fold_in(keys[11], part), 71), part)
    write_logit = draw_write_logit(jax.random.fold_in(jax.random.fold_in(keys[11], part), 71), part)
    output_gate = normal_values(part_splits[5], (CONTEXT_TOKENS, VALUE_HEADS, HD), 1.0, 6.0, ((0, 16),))
    attn_query = draw_attn_query(jax.random.fold_in(jax.random.fold_in(keys[11], part), 71), part)
    attn_key = draw_attn_key(jax.random.fold_in(jax.random.fold_in(keys[11], part), 71), part)
    attn_value = normal_values(part_splits[8], (CONTEXT_TOKENS, KVH, AD), 1.0, 6.0, ((0, 16),))
    attn_gate = normal_values(part_splits[9], (CONTEXT_TOKENS, QH, AD), 1.5, 6.0, ((0, 16),))
    doc_ids = jnp.searchsorted(jnp.cumsum(uneven_parts(part_splits[10], DOCS, NBLK, DOC_BLK, 2)), jnp.arange(NBLK), side="right").astype(jnp.int32)
    return {"delta_query": delta_query, "delta_key": delta_key, "delta_value": delta_value, "log_decay": log_decay, "write_logit": write_logit, "output_gate": output_gate, "attn_query": attn_query, "attn_key": attn_key, "attn_value": attn_value, "attn_gate": attn_gate, "doc_ids": doc_ids}


highest = lax.Precision.HIGHEST

def unit_rows(vectors):
    vectors = vectors.astype(jnp.float32)
    return vectors * lax.rsqrt(lax.optimization_barrier(jnp.sum(vectors * vectors, axis=-1, keepdims=True)) + 1e-06)

def block_terms(queries, key_rows, values, decay_rows, writes):
    length = queries.shape[1]
    head_width = queries.shape[2]
    cumulative = jnp.cumsum(decay_rows, axis=1)
    rowpos = lax.broadcasted_iota(jnp.int32, (length, length), 0)
    colpos = lax.broadcasted_iota(jnp.int32, (length, length), 1)
    spread = cumulative[:, :, None] - cumulative[:, None, :]
    strict = jnp.exp(jnp.where(colpos < rowpos, spread, -jnp.inf))
    inclusive = jnp.exp(jnp.where(colpos <= rowpos, spread, -jnp.inf))
    key_key = jnp.einsum('htd,hsd->hts', key_rows, key_rows, precision=highest)
    query_key = jnp.einsum('htd,hsd->hts', queries, key_rows, precision=highest)
    system = jnp.eye(length, dtype=jnp.float32) + strict * writes[:, None, :] * key_key
    growth = jnp.exp(cumulative)
    stacked = jnp.concatenate([values, growth[:, :, None] * key_rows], axis=2)
    solved = lax.linalg.triangular_solve(system, stacked, left_side=True, lower=True, unit_diagonal=True)
    base_update = solved[:, :, :head_width]
    base_write = solved[:, :, head_width:]
    mixing = inclusive * writes[:, None, :] * query_key
    tail_weight = jnp.exp(cumulative[:, -1:] - cumulative) * writes
    return (growth, mixing, tail_weight, base_update, base_write)

def block_output(block_parts, queries, key_rows, state):
    growth, mixing, tail_weight, base_update, base_write = block_parts
    update = base_update - jnp.einsum('hsk,hvk->hsv', base_write, state, precision=highest)
    outputs = growth[:, :, None] * jnp.einsum('htk,hvk->htv', queries, state, precision=highest)
    outputs = outputs + jnp.einsum('hts,hsv->htv', mixing, update, precision=highest)
    end_state = growth[:, -1, None, None] * state + jnp.einsum('hsv,hsk->hvk', tail_weight[:, :, None] * update, key_rows, precision=highest)
    return (outputs, end_state)

def gated_norm(outputs, gate_rows):
    factor = lax.rsqrt(lax.optimization_barrier(jnp.mean(outputs * outputs, axis=-1, keepdims=True)) + 1e-06)
    return (outputs * factor * jax.nn.silu(gate_rows.astype(jnp.float32))).astype(jnp.bfloat16)

def delta_layer(delta_query, delta_key, delta_value, log_decay, write_logit, output_gate, doc_ids):
    group_ratio = VALUE_HEADS // KH

    def heads_first(tensor):
        return tensor.reshape(NBLK, BLK, VALUE_HEADS, HD).transpose(0, 2, 1, 3)
    queries = heads_first(jnp.repeat(unit_rows(delta_query), group_ratio, axis=1))
    key_rows = heads_first(jnp.repeat(unit_rows(delta_key), group_ratio, axis=1))
    values = heads_first(delta_value.astype(jnp.float32))
    decay_rows = log_decay.reshape(NBLK, BLK, VALUE_HEADS).transpose(0, 2, 1)
    writes = jax.nn.sigmoid(write_logit).reshape(NBLK, BLK, VALUE_HEADS).transpose(0, 2, 1)
    previous = jnp.concatenate([doc_ids[:1] - 1, doc_ids[:-1]])
    carry_mask = (doc_ids == previous).astype(jnp.float32)

    def advance(state, inputs):
        block_q, block_k, block_v, block_g, block_b, block_keep = inputs
        block_parts = block_terms(block_q, block_k, block_v, block_g, block_b)
        outputs, end_state = block_output(block_parts, block_q, block_k, state * block_keep)
        return (end_state, outputs)
    zero_state = jnp.zeros((VALUE_HEADS, HD, HD), jnp.float32)
    unused, outputs = lax.scan(advance, zero_state, (queries, key_rows, values, decay_rows, writes, carry_mask))
    outputs = outputs.transpose(0, 2, 1, 3).reshape(CONTEXT_TOKENS, VALUE_HEADS, HD)
    return gated_norm(outputs, output_gate)

def attention_layer(attn_query, attn_key, attn_value, attn_gate, doc_ids):
    group_size = QH // KVH
    extent_span = SPAN * TOK_DEV
    query_block = min(512, CONTEXT_TOKENS)
    key_span = min(extent_span + query_block, CONTEXT_TOKENS)
    token_docs = jnp.repeat(doc_ids, BLK)

    def attend_block(first):
        key_first = jnp.clip(first - extent_span, 0, CONTEXT_TOKENS - key_span).astype(jnp.int32)
        queries = lax.dynamic_slice_in_dim(attn_query, first, query_block, 0).astype(jnp.float32)
        queries = queries.reshape(query_block, KVH, group_size, AD)
        key_rows = lax.dynamic_slice_in_dim(attn_key, key_first, key_span, 0).astype(jnp.float32)
        value_rows = lax.dynamic_slice_in_dim(attn_value, key_first, key_span, 0).astype(jnp.float32)
        query_pos = first + jnp.arange(query_block, dtype=jnp.int32)
        key_pos = key_first + jnp.arange(key_span, dtype=jnp.int32)
        query_doc = lax.dynamic_slice_in_dim(token_docs, first, query_block)
        key_doc = lax.dynamic_slice_in_dim(token_docs, key_first, key_span)
        allowed = (key_doc[None, :] == query_doc[:, None]) & (key_pos[None, :] <= query_pos[:, None])
        scores = jnp.einsum('tgjd,sgd->gjts', queries, key_rows, precision=highest) * AD ** (-0.5)
        scores = jnp.where(allowed, scores, -jnp.inf)
        weights = jnp.exp(scores - lax.optimization_barrier(jnp.max(scores, axis=-1, keepdims=True)))
        total = lax.optimization_barrier(jnp.sum(weights, axis=-1))
        rounded = lax.optimization_barrier(weights.astype(jnp.bfloat16)).astype(jnp.float32)
        mixed = jnp.einsum('gjts,sgd->tgjd', rounded, value_rows, precision=highest)
        gate_rows = lax.dynamic_slice_in_dim(attn_gate, first, query_block, 0).astype(jnp.float32)
        gate_rows = jax.nn.sigmoid(gate_rows).reshape(query_block, KVH, group_size, AD)
        result = mixed / total.transpose(2, 0, 1)[..., None] * gate_rows
        return result.astype(jnp.bfloat16).reshape(query_block, QH, AD)
    firsts = jnp.arange(CONTEXT_TOKENS // query_block, dtype=jnp.int32) * query_block
    return lax.map(attend_block, firsts).reshape(CONTEXT_TOKENS, QH, AD)

def reference(delta_query, delta_key, delta_value, log_decay, write_logit, output_gate, attn_query, attn_key, attn_value, attn_gate, doc_ids):
    delta_out = delta_layer(delta_query, delta_key, delta_value, log_decay, write_logit, output_gate, doc_ids)
    attn_out = attention_layer(attn_query, attn_key, attn_value, attn_gate, doc_ids)
    return (delta_out, attn_out)
```

```python
import functools

import jax
import jax.numpy as jnp
from jax import lax
from jax.experimental import pallas as pl
from jax.experimental.pallas import tpu as pltpu
from jax.sharding import PartitionSpec as P

BLK = 64
SPAN = 4
F32 = jnp.float32
BF16 = jnp.bfloat16


def mm(a, b):
    return jnp.dot(a, b, preferred_element_type=F32)


def mm_nt(a, b):
    return lax.dot_general(a, b, (((1,), (1,)), ((), ())), preferred_element_type=F32)


def split(x):
    high = x.astype(BF16)
    return high, (x - high.astype(F32)).astype(BF16)


def mm3(a, b):
    ah, al = a
    bh, bl = b
    return mm(ah, bh) + (mm(ah, bl) + mm(al, bh))


def shifted(block, distance):
    devices = range(lax.axis_size("seq"))
    route = [(i - distance, i) for i in devices if i - distance in devices]
    return lax.ppermute(block, "seq", route)


def chunk_kernel(heads, ratio, q_ref, k_ref, v_ref, col_ref, row_ref, incl_ref, maps_ref, base_ref, read_ref):
    length = k_ref.shape[1]
    incl = incl_ref[...] > 0
    rows = lax.broadcasted_iota(jnp.int32, (length, length), 0)
    cols = lax.broadcasted_iota(jnp.int32, (length, length), 1)
    eye = (rows == cols).astype(F32)
    grams = []
    for j in range(heads // ratio):
        k = k_ref[j]
        grams.append((mm_nt(k, k), mm_nt(q_ref[j], k), k.T))
    decays, lows = [], []
    for h in range(heads):
        col = col_ref[0]
        row = row_ref[0]
        c_col, rk_col = col[:, 5 * h : 5 * h + 1], col[:, 5 * h + 1 : 5 * h + 2]
        c_row, bk_row = row[3 * h : 3 * h + 1], row[3 * h + 1 : 3 * h + 2]
        decay = jnp.exp(jnp.where(incl, c_col - c_row, -1e30)) * bk_row
        decays.append(decay)
        lows.append(jnp.where(rows > cols, decay * rk_col * grams[h // ratio][0], 0.0))
    inverses = [eye - jnp.where(rows // 2 == cols // 2, low, 0.0) for low in lows]
    size = 2
    while size < length:
        band = (rows // (2 * size) == cols // (2 * size)) & (rows // size != cols // size)
        parts = [split(x) for x in inverses]
        tops = [mm3(split(jnp.where(band, low, 0.0)), x) for low, x in zip(lows, parts)]
        inverses = [x - mm3(xp, split(t)) for x, xp, t in zip(inverses, parts, tops)]
        size *= 2
    for h in range(heads):
        k_gram, q_gram, k_t = grams[h // ratio]
        k, q, v = k_ref[h // ratio], q_ref[h // ratio], v_ref[h]
        col = col_ref[0]
        rq_col, gq_col, tk_col = (col[:, 5 * h + i : 5 * h + i + 1] for i in (2, 3, 4))
        gain = col_ref[0][length - 1 : length, 5 * heads + h : 5 * heads + h + 1]
        gk_row = row_ref[0][3 * h + 2 : 3 * h + 3]
        th, tl = split(inverses[h])
        update = mm(th, v) + mm(tl, v)
        wh, wl = split(inverses[h] * gk_row)
        write = mm(wh, k) + mm(wl, k)
        both = jnp.concatenate([write, update], axis=1)
        th, tl = split(both * tk_col)
        tail = mm(k_t, th) + mm(k_t, tl)
        maps_ref[h] = jnp.concatenate([eye * gain - tail[:, :length], tail[:, length:]], axis=1).astype(BF16)
        mix = (decays[h] * rq_col * q_gram).astype(BF16)
        mixed = mm(mix, both.astype(BF16))
        base_ref[h] = mixed[:, length:]
        read_ref[h] = (gq_col * q.astype(F32) - mixed[:, :length]).astype(BF16)


def compose_kernel(near_ref, far_ref, map_ref, off_ref, send_ref):
    width = near_ref.shape[1]
    for h in range(near_ref.shape[0]):
        joined = mm(near_ref[h, :, :width], far_ref[h])
        map_ref[h] = joined[:, :width].astype(BF16)
        off = joined[:, width:] + near_ref[h, :, width:].astype(F32)
        off_ref[h] = off
        send_ref[h] = off.astype(BF16)


def output_kernel(base_ref, read_ref, map_ref, off_ref, far_ref, gate_ref, out_ref):
    for h in range(base_ref.shape[0]):
        state = mm(map_ref[h], far_ref[h]) + off_ref[h]
        core = base_ref[h] + mm(read_ref[h], state.astype(BF16))
        factor = lax.rsqrt(jnp.mean(core * core, axis=-1, keepdims=True) + 1e-06)
        gate = gate_ref[h].astype(F32)
        out_ref[h] = (core * factor * (gate / (1.0 + jnp.exp(-gate)))).astype(BF16)


def attention_kernel(scale, runs, q_ref, mask_ref, gate_ref, *refs):
    out_ref = refs[-1]
    keys = jnp.concatenate([r[0, 0] for r in refs[:runs]], axis=0)
    values = jnp.concatenate([r[1, 0] for r in refs[:runs]], axis=0)
    for j in range(q_ref.shape[0]):
        scores = mm_nt(q_ref[j], keys) * scale + mask_ref[...]
        weights = jnp.exp(scores - jnp.max(scores, axis=-1, keepdims=True))
        total = jnp.sum(weights, axis=-1, keepdims=True)
        mixed = mm(weights.astype(BF16), values)
        gate = gate_ref[j].astype(F32)
        out_ref[j] = (mixed / total / (1.0 + jnp.exp(-gate))).astype(BF16)


def local(
    delta_query,
    delta_key,
    delta_value,
    log_decay,
    write_logit,
    output_gate,
    attn_query,
    attn_key,
    attn_value,
    attn_gate,
    doc_ids,
):
    position = lax.axis_index("seq")
    toks, key_heads, width = delta_key.shape
    heads = delta_value.shape[1]
    ratio = heads // key_heads
    blocks = toks // BLK
    kv_heads, attn_width = attn_key.shape[1:]
    query_heads = attn_query.shape[1]
    group = query_heads // kv_heads
    runs = SPAN + 1

    def heads_first(x):
        return x.transpose(1, 0, 2)

    kv = jnp.stack([heads_first(attn_key), heads_first(attn_value)])
    kv_runs = [shifted(kv, d) for d in range(SPAN, 0, -1)] + [kv]

    padded = jnp.concatenate([jnp.full((SPAN * blocks,), -1, doc_ids.dtype), doc_ids])
    window = lax.dynamic_slice_in_dim(padded, position * blocks, runs * blocks)
    key_doc = jnp.repeat(window, BLK)
    tok_doc = key_doc[SPAN * toks :]
    t = jnp.arange(toks, dtype=jnp.int32)
    key_pos = jnp.arange(runs * toks, dtype=jnp.int32) - SPAN * toks
    allowed = (key_doc[None, :] == tok_doc[:, None]) & (key_pos[None, :] <= t[:, None])
    mask = jnp.where(allowed, 0.0, -1e30).astype(F32)
    incl = allowed[:, SPAN * toks :].astype(F32)
    carried = (tok_doc == window[SPAN * blocks - 1]).astype(F32)[:, None]
    lasting = (tok_doc == tok_doc[-1]).astype(F32)[:, None]

    def unit_factor(x):
        x = x.astype(F32)
        return jnp.repeat(lax.rsqrt(jnp.sum(x * x, axis=-1) + 1e-06), ratio, axis=1)

    cum = jnp.cumsum(log_decay, axis=0)
    writes = jax.nn.sigmoid(write_logit)
    rq, rk = unit_factor(delta_query), unit_factor(delta_key)
    grown = jnp.exp(cum) * carried
    tail = jnp.exp(cum[-1:] - cum) * writes * lasting
    per = 4
    steps = heads // per
    cols = jnp.stack([cum, rk, rq, grown * rq, tail * rk], axis=-1)
    cols = cols.reshape(toks, steps, per * 5)
    cols = jnp.concatenate([cols, grown.reshape(toks, steps, per)], axis=-1).transpose(1, 0, 2)
    rowv = jnp.stack([cum, writes * rk, grown * rk], axis=-1)
    rowv = rowv.reshape(toks, steps, per * 3).transpose(1, 2, 0)

    def lead(n, *rest):
        return pl.BlockSpec((n, *rest), lambda i: (i,) + (0,) * len(rest))

    whole = pl.BlockSpec((toks, toks), lambda i: (0, 0))
    params = pltpu.CompilerParams(vmem_limit_bytes=32 * 1024 * 1024)
    maps, base, read = pl.pallas_call(
        functools.partial(chunk_kernel, per, ratio),
        grid=(steps,),
        in_specs=[
            lead(per // ratio, toks, width),
            lead(per // ratio, toks, width),
            lead(per, toks, width),
            lead(1, toks, per * 6),
            lead(1, per * 3, toks),
            whole,
        ],
        out_specs=[lead(per, width, 2 * width), lead(per, toks, width), lead(per, toks, width)],
        out_shape=[
            jax.ShapeDtypeStruct((heads, width, 2 * width), BF16),
            jax.ShapeDtypeStruct((heads, toks, width), F32),
            jax.ShapeDtypeStruct((heads, toks, width), BF16),
        ],
        compiler_params=params,
        cost_estimate=pl.CostEstimate(flops=4 * 10**9, bytes_accessed=4 * 10**6, transcendentals=10**6),
        name="delta_chunk",
    )(heads_first(delta_query), heads_first(delta_key), heads_first(delta_value), cols, rowv, incl)

    near, far = shifted(maps, 1), shifted(maps, 2)

    kv_spec = pl.BlockSpec((2, 1, toks, attn_width), lambda i: (0, i, 0, 0))
    attended = pl.pallas_call(
        functools.partial(attention_kernel, attn_width ** (-0.5), runs),
        grid=(kv_heads,),
        in_specs=[
            lead(group, toks, attn_width),
            pl.BlockSpec(mask.shape, lambda i: (0, 0)),
            lead(group, toks, attn_width),
        ]
        + [kv_spec] * runs,
        out_specs=lead(group, toks, attn_width),
        out_shape=jax.ShapeDtypeStruct((query_heads, toks, attn_width), BF16),
        compiler_params=params,
        cost_estimate=pl.CostEstimate(flops=4 * 10**9, bytes_accessed=4 * 10**6, transcendentals=10**6),
        name="attention",
    )(heads_first(attn_query), mask, heads_first(attn_gate), *kv_runs)

    half = heads // 2
    pair_map, pair_off, pair_send = pl.pallas_call(
        compose_kernel,
        grid=(2,),
        in_specs=[lead(half, width, 2 * width)] * 2,
        out_specs=[lead(half, width, width)] * 3,
        out_shape=[
            jax.ShapeDtypeStruct((heads, width, width), BF16),
            jax.ShapeDtypeStruct((heads, width, width), F32),
            jax.ShapeDtypeStruct((heads, width, width), BF16),
        ],
        compiler_params=params,
        name="compose",
    )(near, far)
    behind = shifted(pair_send, 2)
    delta_out = pl.pallas_call(
        output_kernel,
        grid=(2,),
        in_specs=[lead(half, toks, width)] * 2 + [lead(half, width, width)] * 3 + [lead(half, toks, width)],
        out_specs=lead(half, toks, width),
        out_shape=jax.ShapeDtypeStruct((heads, toks, width), BF16),
        compiler_params=params,
        name="delta_output",
    )(base, read, pair_map, pair_off, behind, heads_first(output_gate))
    return heads_first(delta_out), heads_first(attended)


def solution(mesh):
    tok = P(("groups", "seq"), None, None)
    flat = P(("groups", "seq"), None)
    return jax.shard_map(
        local,
        mesh=mesh,
        in_specs=(tok, tok, tok, flat, flat, tok, tok, tok, tok, tok, P("groups")),
        out_specs=(tok, tok),
        check_vma=False,
    )
```

```python
import functools

import jax
import jax.numpy as jnp
from jax import lax
from jax.experimental import pallas as pl
from jax.experimental.pallas import tpu as pltpu
from jax.sharding import PartitionSpec as P

BLK = 64
SPAN = 4
F32 = jnp.float32
BF16 = jnp.bfloat16
MESH = pl.DeviceIdType.MESH


def mm(a, b):
    return jnp.dot(a, b, preferred_element_type=F32)


def mm_nt(a, b):
    return lax.dot_general(a, b, (((1,), (1,)), ((), ())), preferred_element_type=F32)


def split(x):
    high = x.astype(BF16)
    return high, (x - high.astype(F32)).astype(BF16)


def mm3(a, b):
    ah, al = a
    bh, bl = b
    return mm(ah, bh) + (mm(ah, bl) + mm(al, bh))


def chunk_step(i, heads, ratio, q_ref, k_ref, v_ref, col_ref, row_ref, incl_ref, map_ref, off_ref, base_ref, read_ref, send_ref):
    length = k_ref.shape[1]
    pairs = heads // ratio
    col, row = col_ref[i], row_ref[i]
    incl = incl_ref[...] > 0
    rows = lax.broadcasted_iota(jnp.int32, (length, length), 0)
    cols = lax.broadcasted_iota(jnp.int32, (length, length), 1)
    eye = (rows == cols).astype(F32)
    grams = []
    for j in range(heads // ratio):
        k = k_ref[i * pairs + j]
        grams.append((mm_nt(k, k), mm_nt(q_ref[i * pairs + j], k), k.T))
    decays, lows = [], []
    for h in range(heads):
        c_col, rk_col = col[:, 5 * h : 5 * h + 1], col[:, 5 * h + 1 : 5 * h + 2]
        c_row, bk_row = row[3 * h : 3 * h + 1], row[3 * h + 1 : 3 * h + 2]
        decay = jnp.exp(jnp.where(incl, c_col - c_row, -1e30)) * bk_row
        decays.append(decay)
        lows.append(jnp.where(rows > cols, decay * rk_col * grams[h // ratio][0], 0.0))
    inverses = [eye - jnp.where(rows // 2 == cols // 2, low, 0.0) for low in lows]
    size = 2
    while size < length:
        band = (rows // (2 * size) == cols // (2 * size)) & (rows // size != cols // size)
        parts = [split(x) for x in inverses]
        tops = [mm3(split(jnp.where(band, low, 0.0)), x) for low, x in zip(lows, parts)]
        inverses = [x - mm3(xp, split(t)) for x, xp, t in zip(inverses, parts, tops)]
        size *= 2
    for h in range(heads):
        k_gram, q_gram, k_t = grams[h // ratio]
        k, q, v = k_ref[i * pairs + h // ratio], q_ref[i * pairs + h // ratio], v_ref[i * heads + h]
        rq_col, gq_col, tk_col = (col[:, 5 * h + n : 5 * h + n + 1] for n in (2, 3, 4))
        gain = col[length - 1 : length, 5 * heads + h : 5 * heads + h + 1]
        gk_row = row[3 * h + 2 : 3 * h + 3]
        th, tl = split(inverses[h])
        update = mm(th, v) + mm(tl, v)
        wh, wl = split(inverses[h] * gk_row)
        write = mm(wh, k) + mm(wl, k)
        both = jnp.concatenate([write, update], axis=1)
        th, tl = split(both * tk_col)
        tail = mm(k_t, th) + mm(k_t, tl)
        map_ref[i, h] = (eye * gain - tail[:, :length]).astype(BF16)
        off_ref[i, h] = tail[:, length:]
        send_ref[0, i, h] = tail[:, length:].astype(BF16)
        mix = (decays[h] * rq_col * q_gram).astype(BF16)
        mixed = mm(mix, both.astype(BF16))
        base_ref[i, h] = mixed[:, length:]
        read_ref[i, h] = (gq_col * q.astype(F32) - mixed[:, :length]).astype(BF16)


def layer_kernel(
    per,
    ratio,
    scale,
    q_ref,
    k_ref,
    v_ref,
    col_ref,
    row_ref,
    incl_ref,
    gate_ref,
    kv_ref,
    aq_ref,
    mask_ref,
    agate_ref,
    out_ref,
    att_ref,
    kv_in,
    map_ref,
    off_ref,
    base_ref,
    read_ref,
    send_ref,
    recv_ref,
    kv_send_sem,
    kv_recv_sem,
    send_sem,
    recv_sem,
):
    size = lax.axis_size("seq")
    me = lax.axis_index("seq")
    steps = map_ref.shape[0]

    def device(d):
        return {"seq": lax.rem(me + d + size, size)}

    barrier = pltpu.get_barrier_semaphore()
    for d in range(1, SPAN + 1):
        for side in (d, -d):
            pl.semaphore_signal(barrier, inc=1, device_id=device(side), device_id_type=MESH)
    pl.semaphore_wait(barrier, 2 * SPAN)

    def kv_copy(d):
        return pltpu.make_async_remote_copy(
            src_ref=kv_ref,
            dst_ref=kv_in.at[d - 1],
            send_sem=kv_send_sem.at[d - 1],
            recv_sem=kv_recv_sem.at[d - 1],
            device_id=device(d),
            device_id_type=MESH,
        )

    def hop_copy(hop, i):
        return pltpu.make_async_remote_copy(
            src_ref=send_ref.at[hop, i],
            dst_ref=recv_ref.at[hop, i],
            send_sem=send_sem.at[hop, i],
            recv_sem=recv_sem.at[hop, i],
            device_id=device(1),
            device_id_type=MESH,
        )

    for d in range(1, SPAN + 1):
        kv_copy(d).start()

    @pl.loop(0, steps)
    def _(i):
        chunk_step(
            i, per, ratio, q_ref, k_ref, v_ref, col_ref, row_ref, incl_ref, map_ref, off_ref, base_ref, read_ref, send_ref
        )
        hop_copy(0, i).start()

    for d in range(1, SPAN + 1):
        kv_copy(d).wait_recv()
    group = aq_ref.shape[0] // kv_ref.shape[1]

    @pl.loop(0, kv_ref.shape[1])
    def _(g):
        keys = jnp.concatenate([kv_in[d - 1, 0, g] for d in range(SPAN, 0, -1)] + [kv_ref[0, g]], axis=0)
        values = jnp.concatenate([kv_in[d - 1, 1, g] for d in range(SPAN, 0, -1)] + [kv_ref[1, g]], axis=0)
        for j in range(group):
            scores = mm_nt(aq_ref[g * group + j], keys) * scale + mask_ref[...]
            weights = jnp.exp(scores - jnp.max(scores, axis=-1, keepdims=True))
            total = jnp.sum(weights, axis=-1, keepdims=True)
            mixed = mm(weights.astype(BF16), values)
            gate = agate_ref[g * group + j].astype(F32)
            att_ref[g * group + j] = (mixed / total / (1.0 + jnp.exp(-gate))).astype(BF16)

    @pl.loop(0, (SPAN - 1) * steps)
    def _(r):
        hop, i = r // steps, r % steps
        hop_copy(hop, i).wait_recv()
        for h in range(per):
            state = mm(map_ref[i, h], recv_ref[hop, i, h]) + off_ref[i, h]
            send_ref[hop + 1, i, h] = state.astype(BF16)
        hop_copy(hop + 1, i).start()

    @pl.loop(0, steps)
    def _(i):
        hop_copy(SPAN - 1, i).wait_recv()
        for h in range(per):
            core = base_ref[i, h] + mm(read_ref[i, h], recv_ref[SPAN - 1, i, h])
            factor = lax.rsqrt(jnp.mean(core * core, axis=-1, keepdims=True) + 1e-06)
            gate = gate_ref[i * per + h].astype(F32)
            out_ref[i * per + h] = (core * factor * (gate / (1.0 + jnp.exp(-gate)))).astype(BF16)

    for d in range(1, SPAN + 1):
        kv_copy(d).wait_send()

    @pl.loop(0, SPAN * steps)
    def _(r):
        hop_copy(r // steps, r % steps).wait_send()


def local(
    delta_query,
    delta_key,
    delta_value,
    log_decay,
    write_logit,
    output_gate,
    attn_query,
    attn_key,
    attn_value,
    attn_gate,
    doc_ids,
):
    position = lax.axis_index("seq")
    toks, key_heads, width = delta_key.shape
    heads = delta_value.shape[1]
    ratio = heads // key_heads
    blocks = toks // BLK
    kv_heads, attn_width = attn_key.shape[1:]
    query_heads = attn_query.shape[1]
    group = query_heads // kv_heads
    runs = SPAN + 1

    def heads_first(x):
        return x.transpose(1, 0, 2)

    kv = jnp.stack([heads_first(attn_key), heads_first(attn_value)])

    padded = jnp.concatenate([jnp.full((SPAN * blocks,), -1, doc_ids.dtype), doc_ids])
    window = lax.dynamic_slice_in_dim(padded, position * blocks, runs * blocks)
    key_doc = jnp.repeat(window, BLK)
    tok_doc = key_doc[SPAN * toks :]
    t = jnp.arange(toks, dtype=jnp.int32)
    key_pos = jnp.arange(runs * toks, dtype=jnp.int32) - SPAN * toks
    allowed = (key_doc[None, :] == tok_doc[:, None]) & (key_pos[None, :] <= t[:, None])
    mask = jnp.where(allowed, 0.0, -1e30).astype(F32)
    incl = allowed[:, SPAN * toks :].astype(F32)
    carried = (tok_doc == window[SPAN * blocks - 1]).astype(F32)[:, None]
    lasting = (tok_doc == tok_doc[-1]).astype(F32)[:, None]

    def unit_factor(x):
        x = x.astype(F32)
        return jnp.repeat(lax.rsqrt(jnp.sum(x * x, axis=-1) + 1e-06), ratio, axis=1)

    cum = jnp.cumsum(log_decay, axis=0)
    writes = jax.nn.sigmoid(write_logit)
    rq, rk = unit_factor(delta_query), unit_factor(delta_key)
    grown = jnp.exp(cum) * carried
    tail = jnp.exp(cum[-1:] - cum) * writes * lasting
    per = 4
    steps = heads // per
    cols = jnp.stack([cum, rk, rq, grown * rq, tail * rk], axis=-1)
    cols = cols.reshape(toks, steps, per * 5)
    cols = jnp.concatenate([cols, grown.reshape(toks, steps, per)], axis=-1).transpose(1, 0, 2)
    rowv = jnp.stack([cum, writes * rk, grown * rk], axis=-1)
    rowv = rowv.reshape(toks, steps, per * 3).transpose(1, 2, 0)

    delta_out, attended = pl.pallas_call(
        functools.partial(layer_kernel, per, ratio, attn_width ** (-0.5)),
        in_specs=[pl.BlockSpec(memory_space=pltpu.VMEM)] * 11,
        out_specs=[pl.BlockSpec(memory_space=pltpu.VMEM)] * 2,
        out_shape=[
            jax.ShapeDtypeStruct((heads, toks, width), BF16),
            jax.ShapeDtypeStruct((query_heads, toks, attn_width), BF16),
        ],
        scratch_shapes=[
            pltpu.VMEM((SPAN, 2, kv_heads, toks, attn_width), BF16),
            pltpu.VMEM((steps, per, width, width), BF16),
            pltpu.VMEM((steps, per, width, width), F32),
            pltpu.VMEM((steps, per, toks, width), F32),
            pltpu.VMEM((steps, per, toks, width), BF16),
            pltpu.VMEM((SPAN, steps, per, width, width), BF16),
            pltpu.VMEM((SPAN, steps, per, width, width), BF16),
            pltpu.SemaphoreType.DMA((SPAN,)),
            pltpu.SemaphoreType.DMA((SPAN,)),
            pltpu.SemaphoreType.DMA((SPAN, steps)),
            pltpu.SemaphoreType.DMA((SPAN, steps)),
        ],
        compiler_params=pltpu.CompilerParams(
            collective_id=0, has_side_effects=True, vmem_limit_bytes=48 * 1024 * 1024
        ),
        cost_estimate=pl.CostEstimate(flops=8 * 10**9, bytes_accessed=8 * 10**6, transcendentals=2 * 10**6),
        name="layer",
    )(
        heads_first(delta_query),
        heads_first(delta_key),
        heads_first(delta_value),
        cols,
        rowv,
        incl,
        heads_first(output_gate),
        kv,
        heads_first(attn_query),
        mask,
        heads_first(attn_gate),
    )
    return heads_first(delta_out), heads_first(attended)


def solution(mesh):
    tok = P(("groups", "seq"), None, None)
    flat = P(("groups", "seq"), None)
    return jax.shard_map(
        local,
        mesh=mesh,
        in_specs=(tok, tok, tok, flat, flat, tok, tok, tok, tok, tok, P("groups")),
        out_specs=(tok, tok),
        check_vma=False,
    )
```

```python
import functools

import jax
import jax.numpy as jnp
from jax import lax
from jax.experimental import pallas as pl
from jax.experimental.pallas import tpu as pltpu
from jax.sharding import PartitionSpec as P

BLK = 64
SPAN = 4
F32 = jnp.float32
BF16 = jnp.bfloat16
MESH = pl.DeviceIdType.MESH


def mm(a, b):
    return jnp.dot(a, b, preferred_element_type=F32)


def mm_nt(a, b):
    return lax.dot_general(a, b, (((1,), (1,)), ((), ())), preferred_element_type=F32)


def split(x):
    high = x.astype(BF16)
    return high, (x - high.astype(F32)).astype(BF16)


def mm3(a, b):
    ah, al = a
    bh, bl = b
    return mm(ah, bh) + (mm(ah, bl) + mm(al, bh))


def chunk_step(i, heads, ratio, q_ref, k_ref, v_ref, col_ref, row_ref, incl_ref, map_ref, off_ref, base_ref, read_ref, send_ref):
    length = k_ref.shape[1]
    pairs = heads // ratio
    col, row = col_ref[i], row_ref[i]
    incl = incl_ref[...] > 0
    rows = lax.broadcasted_iota(jnp.int32, (length, length), 0)
    cols = lax.broadcasted_iota(jnp.int32, (length, length), 1)
    eye = (rows == cols).astype(F32)
    grams = []
    for j in range(heads // ratio):
        k = k_ref[i * pairs + j]
        grams.append((mm_nt(k, k), mm_nt(q_ref[i * pairs + j], k), k.T))
    decays, lows = [], []
    for h in range(heads):
        c_col, rk_col = col[:, 5 * h : 5 * h + 1], col[:, 5 * h + 1 : 5 * h + 2]
        c_row, bk_row = row[3 * h : 3 * h + 1], row[3 * h + 1 : 3 * h + 2]
        decay = jnp.exp(jnp.where(incl, c_col - c_row, -1e30)) * bk_row
        decays.append(decay)
        lows.append(jnp.where(rows > cols, decay * rk_col * grams[h // ratio][0], 0.0))
    inverses = [eye - jnp.where(rows // 2 == cols // 2, low, 0.0) for low in lows]
    size = 2
    while size < length:
        band = (rows // (2 * size) == cols // (2 * size)) & (rows // size != cols // size)
        parts = [split(x) for x in inverses]
        tops = [mm3(split(jnp.where(band, low, 0.0)), x) for low, x in zip(lows, parts)]
        inverses = [x - mm3(xp, split(t)) for x, xp, t in zip(inverses, parts, tops)]
        size *= 2
    for h in range(heads):
        k_gram, q_gram, k_t = grams[h // ratio]
        k, q, v = k_ref[i * pairs + h // ratio], q_ref[i * pairs + h // ratio], v_ref[i * heads + h]
        rq_col, gq_col, tk_col = (col[:, 5 * h + n : 5 * h + n + 1] for n in (2, 3, 4))
        gain = col[length - 1 : length, 5 * heads + h : 5 * heads + h + 1]
        gk_row = row[3 * h + 2 : 3 * h + 3]
        th, tl = split(inverses[h])
        update = mm(th, v) + mm(tl, v)
        wh, wl = split(inverses[h] * gk_row)
        write = mm(wh, k) + mm(wl, k)
        both = jnp.concatenate([write, update], axis=1)
        th, tl = split(both * tk_col)
        tail = mm(k_t, th) + mm(k_t, tl)
        map_ref[i, h] = (eye * gain - tail[:, :length]).astype(BF16)
        off_ref[i, h] = tail[:, length:]
        send_ref[0, i, h] = tail[:, length:].astype(BF16)
        mix = (decays[h] * rq_col * q_gram).astype(BF16)
        mixed = mm(mix, both.astype(BF16))
        base_ref[i, h] = mixed[:, length:]
        read_ref[i, h] = (gq_col * q.astype(F32) - mixed[:, :length]).astype(BF16)


def layer_kernel(
    per,
    ratio,
    scale,
    q_ref,
    k_ref,
    v_ref,
    col_ref,
    row_ref,
    incl_ref,
    gate_ref,
    kv_ref,
    aq_ref,
    mask_ref,
    agate_ref,
    out_ref,
    att_ref,
    kv_in,
    map_ref,
    off_ref,
    base_ref,
    read_ref,
    send_ref,
    recv_ref,
    kv_send_sem,
    kv_recv_sem,
    send_sem,
    recv_sem,
):
    size = lax.axis_size("seq")
    me = lax.axis_index("seq")
    steps = map_ref.shape[0]

    def device(d):
        return {"seq": lax.rem(me + d + size, size)}

    barrier = pltpu.get_barrier_semaphore()
    place = lax.rem(me, SPAN)

    def fellow(r):
        return {"seq": me - place + lax.rem(place + r, SPAN)}

    greeted = [device(d) for d in (1, -1, SPAN, -SPAN)] + [fellow(r) for r in range(1, SPAN)]
    for other in greeted:
        pl.semaphore_signal(barrier, inc=1, device_id=other, device_id_type=MESH)
    pl.semaphore_wait(barrier, len(greeted))

    def kv_copy(d, source):
        return pltpu.make_async_remote_copy(
            src_ref=source,
            dst_ref=kv_in.at[d - 1],
            send_sem=kv_send_sem.at[d - 1],
            recv_sem=kv_recv_sem.at[d - 1],
            device_id=device(SPAN) if d == SPAN else fellow(d),
            device_id_type=MESH,
        )

    def hop_copy(hop, i):
        return pltpu.make_async_remote_copy(
            src_ref=send_ref.at[hop, i],
            dst_ref=recv_ref.at[hop, i],
            send_sem=send_sem.at[hop, i],
            recv_sem=recv_sem.at[hop, i],
            device_id=device(1),
            device_id_type=MESH,
        )

    def advance(t):
        for hop in range(SPAN - 1):
            i = t - 1 - hop

            @pl.when((i >= 0) & (i < steps))
            def _():
                hop_copy(hop, i).wait_recv()
                for h in range(per):
                    state = mm(map_ref[i, h], recv_ref[hop, i, h]) + off_ref[i, h]
                    send_ref[hop + 1, i, h] = state.astype(BF16)
                hop_copy(hop + 1, i).start()

    kv_copy(SPAN, kv_ref).start()
    for d in range(1, SPAN):

        @pl.when(place + d < SPAN)
        def _(d=d):
            kv_copy(d, kv_ref).start()

    @pl.loop(0, steps)
    def _(i):
        chunk_step(
            i, per, ratio, q_ref, k_ref, v_ref, col_ref, row_ref, incl_ref, map_ref, off_ref, base_ref, read_ref, send_ref
        )
        hop_copy(0, i).start()

        @pl.when(i == 1)
        def _():
            kv_copy(SPAN, kv_ref).wait_recv()
            for d in range(1, SPAN):

                @pl.when(place + d >= SPAN)
                def _(d=d):
                    kv_copy(d, kv_in.at[SPAN - 1]).start()

        advance(i)

    for d in range(1, SPAN):
        kv_copy(d, kv_ref).wait_recv()
    group = aq_ref.shape[0] // kv_ref.shape[1]

    @pl.loop(0, kv_ref.shape[1])
    def _(g):
        keys = jnp.concatenate([kv_in[d - 1, 0, g] for d in range(SPAN, 0, -1)] + [kv_ref[0, g]], axis=0)
        values = jnp.concatenate([kv_in[d - 1, 1, g] for d in range(SPAN, 0, -1)] + [kv_ref[1, g]], axis=0)
        for j in range(group):
            scores = mm_nt(aq_ref[g * group + j], keys) * scale + mask_ref[...]
            weights = jnp.exp(scores - jnp.max(scores, axis=-1, keepdims=True))
            total = jnp.sum(weights, axis=-1, keepdims=True)
            mixed = mm(weights.astype(BF16), values)
            gate = agate_ref[g * group + j].astype(F32)
            att_ref[g * group + j] = (mixed / total / (1.0 + jnp.exp(-gate))).astype(BF16)

    @pl.loop(SPAN, steps + SPAN)
    def _(t):
        advance(t)
        i = t - SPAN
        hop_copy(SPAN - 1, i).wait_recv()
        for h in range(per):
            core = base_ref[i, h] + mm(read_ref[i, h], recv_ref[SPAN - 1, i, h])
            factor = lax.rsqrt(jnp.mean(core * core, axis=-1, keepdims=True) + 1e-06)
            gate = gate_ref[i * per + h].astype(F32)
            out_ref[i * per + h] = (core * factor * (gate / (1.0 + jnp.exp(-gate)))).astype(BF16)

    for d in range(1, SPAN + 1):
        kv_copy(d, kv_ref).wait_send()

    @pl.loop(0, SPAN * steps)
    def _(r):
        hop_copy(r // steps, r % steps).wait_send()


def local(
    delta_query,
    delta_key,
    delta_value,
    log_decay,
    write_logit,
    output_gate,
    attn_query,
    attn_key,
    attn_value,
    attn_gate,
    doc_ids,
):
    position = lax.axis_index("seq")
    toks, key_heads, width = delta_key.shape
    heads = delta_value.shape[1]
    ratio = heads // key_heads
    blocks = toks // BLK
    kv_heads, attn_width = attn_key.shape[1:]
    query_heads = attn_query.shape[1]
    group = query_heads // kv_heads
    runs = SPAN + 1

    def heads_first(x):
        return x.transpose(1, 0, 2)

    kv = jnp.stack([heads_first(attn_key), heads_first(attn_value)])

    padded = jnp.concatenate([jnp.full((SPAN * blocks,), -1, doc_ids.dtype), doc_ids])
    window = lax.dynamic_slice_in_dim(padded, position * blocks, runs * blocks)
    key_doc = jnp.repeat(window, BLK)
    tok_doc = key_doc[SPAN * toks :]
    t = jnp.arange(toks, dtype=jnp.int32)
    key_pos = jnp.arange(runs * toks, dtype=jnp.int32) - SPAN * toks
    allowed = (key_doc[None, :] == tok_doc[:, None]) & (key_pos[None, :] <= t[:, None])
    mask = jnp.where(allowed, 0.0, -1e30).astype(F32)
    incl = allowed[:, SPAN * toks :].astype(F32)
    carried = (tok_doc == window[SPAN * blocks - 1]).astype(F32)[:, None]
    lasting = (tok_doc == tok_doc[-1]).astype(F32)[:, None]

    def unit_factor(x):
        x = x.astype(F32)
        return jnp.repeat(lax.rsqrt(jnp.sum(x * x, axis=-1) + 1e-06), ratio, axis=1)

    cum = jnp.cumsum(log_decay, axis=0)
    writes = jax.nn.sigmoid(write_logit)
    rq, rk = unit_factor(delta_query), unit_factor(delta_key)
    grown = jnp.exp(cum) * carried
    tail = jnp.exp(cum[-1:] - cum) * writes * lasting
    per = 4
    steps = heads // per
    cols = jnp.stack([cum, rk, rq, grown * rq, tail * rk], axis=-1)
    cols = cols.reshape(toks, steps, per * 5)
    cols = jnp.concatenate([cols, grown.reshape(toks, steps, per)], axis=-1).transpose(1, 0, 2)
    rowv = jnp.stack([cum, writes * rk, grown * rk], axis=-1)
    rowv = rowv.reshape(toks, steps, per * 3).transpose(1, 2, 0)

    delta_out, attended = pl.pallas_call(
        functools.partial(layer_kernel, per, ratio, attn_width ** (-0.5)),
        in_specs=[pl.BlockSpec(memory_space=pltpu.VMEM)] * 11,
        out_specs=[pl.BlockSpec(memory_space=pltpu.VMEM)] * 2,
        out_shape=[
            jax.ShapeDtypeStruct((heads, toks, width), BF16),
            jax.ShapeDtypeStruct((query_heads, toks, attn_width), BF16),
        ],
        scratch_shapes=[
            pltpu.VMEM((SPAN, 2, kv_heads, toks, attn_width), BF16),
            pltpu.VMEM((steps, per, width, width), BF16),
            pltpu.VMEM((steps, per, width, width), F32),
            pltpu.VMEM((steps, per, toks, width), F32),
            pltpu.VMEM((steps, per, toks, width), BF16),
            pltpu.VMEM((SPAN, steps, per, width, width), BF16),
            pltpu.VMEM((SPAN, steps, per, width, width), BF16),
            pltpu.SemaphoreType.DMA((SPAN,)),
            pltpu.SemaphoreType.DMA((SPAN,)),
            pltpu.SemaphoreType.DMA((SPAN, steps)),
            pltpu.SemaphoreType.DMA((SPAN, steps)),
        ],
        compiler_params=pltpu.CompilerParams(
            collective_id=0, has_side_effects=True, vmem_limit_bytes=48 * 1024 * 1024
        ),
        cost_estimate=pl.CostEstimate(flops=8 * 10**9, bytes_accessed=8 * 10**6, transcendentals=2 * 10**6),
        name="layer",
    )(
        heads_first(delta_query),
        heads_first(delta_key),
        heads_first(delta_value),
        cols,
        rowv,
        incl,
        heads_first(output_gate),
        kv,
        heads_first(attn_query),
        mask,
        heads_first(attn_gate),
    )
    return heads_first(delta_out), heads_first(attended)


def solution(mesh):
    tok = P(("groups", "seq"), None, None)
    flat = P(("groups", "seq"), None)
    return jax.shard_map(
        local,
        mesh=mesh,
        in_specs=(tok, tok, tok, flat, flat, tok, tok, tok, tok, tok, P("groups")),
        out_specs=(tok, tok),
        check_vma=False,
    )
```

```python
import functools

import jax
import jax.numpy as jnp
from jax import lax
from jax.experimental import pallas as pl
from jax.experimental.pallas import tpu as pltpu
from jax.sharding import PartitionSpec as P

BLK = 64
SPAN = 4
F32 = jnp.float32
BF16 = jnp.bfloat16
MESH = pl.DeviceIdType.MESH


def mm(a, b):
    return jnp.dot(a, b, preferred_element_type=F32)


def mm_nt(a, b):
    return lax.dot_general(a, b, (((1,), (1,)), ((), ())), preferred_element_type=F32)


def split(x):
    high = x.astype(BF16)
    return high, (x - high.astype(F32)).astype(BF16)


def mm3(a, b):
    ah, al = a
    bh, bl = b
    return mm(ah, bh) + (mm(ah, bl) + mm(al, bh))


def chunk_step(i, heads, ratio, q_ref, k_ref, v_ref, col_ref, row_ref, incl_ref, map_ref, off_ref, base_ref, read_ref, send_ref):
    length = k_ref.shape[1]
    pairs = heads // ratio
    col, row = col_ref[i], row_ref[i]
    incl = incl_ref[...] > 0
    rows = lax.broadcasted_iota(jnp.int32, (length, length), 0)
    cols = lax.broadcasted_iota(jnp.int32, (length, length), 1)
    eye = (rows == cols).astype(F32)
    grams = []
    for j in range(heads // ratio):
        k = k_ref[i * pairs + j]
        grams.append((mm_nt(k, k), mm_nt(q_ref[i * pairs + j], k), k.T))
    decays, lows = [], []
    for h in range(heads):
        c_col, rk_col = col[:, 5 * h : 5 * h + 1], col[:, 5 * h + 1 : 5 * h + 2]
        c_row, bk_row = row[3 * h : 3 * h + 1], row[3 * h + 1 : 3 * h + 2]
        decay = jnp.exp(jnp.where(incl, c_col - c_row, -1e30)) * bk_row
        decays.append(decay)
        lows.append(jnp.where(rows > cols, decay * rk_col * grams[h // ratio][0], 0.0))
    inverses = [eye - jnp.where(rows // 2 == cols // 2, low, 0.0) for low in lows]
    size = 2
    while size < length:
        band = (rows // (2 * size) == cols // (2 * size)) & (rows // size != cols // size)
        parts = [split(x) for x in inverses]
        tops = [mm3(split(jnp.where(band, low, 0.0)), x) for low, x in zip(lows, parts)]
        inverses = [x - mm3(xp, split(t)) for x, xp, t in zip(inverses, parts, tops)]
        size *= 2
    for h in range(heads):
        k_gram, q_gram, k_t = grams[h // ratio]
        k, q, v = k_ref[i * pairs + h // ratio], q_ref[i * pairs + h // ratio], v_ref[i * heads + h]
        rq_col, gq_col, tk_col = (col[:, 5 * h + n : 5 * h + n + 1] for n in (2, 3, 4))
        gain = col[length - 1 : length, 5 * heads + h : 5 * heads + h + 1]
        gk_row = row[3 * h + 2 : 3 * h + 3]
        th, tl = split(inverses[h])
        update = mm(th, v) + mm(tl, v)
        wh, wl = split(inverses[h] * gk_row)
        write = mm(wh, k) + mm(wl, k)
        both = jnp.concatenate([write, update], axis=1)
        th, tl = split(both * tk_col)
        tail = mm(k_t, th) + mm(k_t, tl)
        map_ref[i, h] = (eye * gain - tail[:, :length]).astype(BF16)
        off_ref[i, h] = tail[:, length:]
        send_ref[0, i, h] = tail[:, length:].astype(BF16)
        mix = (decays[h] * rq_col * q_gram).astype(BF16)
        mixed = mm(mix, both.astype(BF16))
        base_ref[i, h] = mixed[:, length:]
        read_ref[i, h] = (gq_col * q.astype(F32) - mixed[:, :length]).astype(BF16)


def layer_kernel(
    per,
    ratio,
    scale,
    q_ref,
    k_ref,
    v_ref,
    col_ref,
    row_ref,
    incl_ref,
    gate_ref,
    kv_ref,
    aq_ref,
    mask_ref,
    agate_ref,
    out_ref,
    att_ref,
    kv_in,
    map_ref,
    off_ref,
    base_ref,
    read_ref,
    send_ref,
    recv_ref,
    kv_send_sem,
    kv_recv_sem,
    send_sem,
    recv_sem,
):
    size = lax.axis_size("seq")
    me = lax.axis_index("seq")
    steps = map_ref.shape[0]

    def device(d):
        return {"seq": lax.rem(me + d + size, size)}

    barrier = pltpu.get_barrier_semaphore()
    for d in range(1, SPAN + 1):
        for side in (d, -d):
            pl.semaphore_signal(barrier, inc=1, device_id=device(side), device_id_type=MESH)
    pl.semaphore_wait(barrier, 2 * SPAN)

    def kv_copy(d):
        return pltpu.make_async_remote_copy(
            src_ref=kv_ref,
            dst_ref=kv_in.at[d - 1],
            send_sem=kv_send_sem.at[d - 1],
            recv_sem=kv_recv_sem.at[d - 1],
            device_id=device(d),
            device_id_type=MESH,
        )

    def hop_copy(hop, i):
        return pltpu.make_async_remote_copy(
            src_ref=send_ref.at[hop, i],
            dst_ref=recv_ref.at[hop, i],
            send_sem=send_sem.at[hop, i],
            recv_sem=recv_sem.at[hop, i],
            device_id=device(1),
            device_id_type=MESH,
        )

    for d in range(1, SPAN + 1):

        @pl.when(me + d < size)
        def _(d=d):
            kv_copy(d).start()

        @pl.when(me < d)
        def _(d=d):
            kv_in[d - 1] = jnp.zeros(kv_in.shape[1:], BF16)

    @pl.when(me == 0)
    def _():
        @pl.loop(0, SPAN * steps)
        def _(r):
            recv_ref[r // steps, r % steps] = jnp.zeros(recv_ref.shape[2:], BF16)

    @pl.loop(0, steps)
    def _(i):
        chunk_step(
            i, per, ratio, q_ref, k_ref, v_ref, col_ref, row_ref, incl_ref, map_ref, off_ref, base_ref, read_ref, send_ref
        )

        @pl.when(me + 1 < size)
        def _():
            hop_copy(0, i).start()

    for d in range(1, SPAN + 1):

        @pl.when(me >= d)
        def _(d=d):
            kv_copy(d).wait_recv()

    group = aq_ref.shape[0] // kv_ref.shape[1]

    @pl.loop(0, kv_ref.shape[1])
    def _(g):
        keys = jnp.concatenate([kv_in[d - 1, 0, g] for d in range(SPAN, 0, -1)] + [kv_ref[0, g]], axis=0)
        values = jnp.concatenate([kv_in[d - 1, 1, g] for d in range(SPAN, 0, -1)] + [kv_ref[1, g]], axis=0)
        for j in range(group):
            scores = mm_nt(aq_ref[g * group + j], keys) * scale + mask_ref[...]
            weights = jnp.exp(scores - jnp.max(scores, axis=-1, keepdims=True))
            total = jnp.sum(weights, axis=-1, keepdims=True)
            mixed = mm(weights.astype(BF16), values)
            gate = agate_ref[g * group + j].astype(F32)
            att_ref[g * group + j] = (mixed / total / (1.0 + jnp.exp(-gate))).astype(BF16)

    @pl.loop(0, (SPAN - 1) * steps)
    def _(r):
        hop, i = r // steps, r % steps

        @pl.when(me > 0)
        def _():
            hop_copy(hop, i).wait_recv()

        for h in range(per):
            state = mm(map_ref[i, h], recv_ref[hop, i, h]) + off_ref[i, h]
            send_ref[hop + 1, i, h] = state.astype(BF16)

        @pl.when(me + 1 < size)
        def _():
            hop_copy(hop + 1, i).start()

    @pl.loop(0, steps)
    def _(i):

        @pl.when(me > 0)
        def _():
            hop_copy(SPAN - 1, i).wait_recv()

        for h in range(per):
            core = base_ref[i, h] + mm(read_ref[i, h], recv_ref[SPAN - 1, i, h])
            factor = lax.rsqrt(jnp.mean(core * core, axis=-1, keepdims=True) + 1e-06)
            gate = gate_ref[i * per + h].astype(F32)
            out_ref[i * per + h] = (core * factor * (gate / (1.0 + jnp.exp(-gate)))).astype(BF16)

    for d in range(1, SPAN + 1):

        @pl.when(me + d < size)
        def _(d=d):
            kv_copy(d).wait_send()

    @pl.when(me + 1 < size)
    def _():
        @pl.loop(0, SPAN * steps)
        def _(r):
            hop_copy(r // steps, r % steps).wait_send()


def local(
    delta_query,
    delta_key,
    delta_value,
    log_decay,
    write_logit,
    output_gate,
    attn_query,
    attn_key,
    attn_value,
    attn_gate,
    doc_ids,
):
    position = lax.axis_index("seq")
    toks, key_heads, width = delta_key.shape
    heads = delta_value.shape[1]
    ratio = heads // key_heads
    blocks = toks // BLK
    kv_heads, attn_width = attn_key.shape[1:]
    query_heads = attn_query.shape[1]
    group = query_heads // kv_heads
    runs = SPAN + 1

    def heads_first(x):
        return x.transpose(1, 0, 2)

    kv = jnp.stack([heads_first(attn_key), heads_first(attn_value)])

    padded = jnp.concatenate([jnp.full((SPAN * blocks,), -1, doc_ids.dtype), doc_ids])
    window = lax.dynamic_slice_in_dim(padded, position * blocks, runs * blocks)
    key_doc = jnp.repeat(window, BLK)
    tok_doc = key_doc[SPAN * toks :]
    t = jnp.arange(toks, dtype=jnp.int32)
    key_pos = jnp.arange(runs * toks, dtype=jnp.int32) - SPAN * toks
    allowed = (key_doc[None, :] == tok_doc[:, None]) & (key_pos[None, :] <= t[:, None])
    mask = jnp.where(allowed, 0.0, -1e30).astype(F32)
    incl = allowed[:, SPAN * toks :].astype(F32)
    carried = (tok_doc == window[SPAN * blocks - 1]).astype(F32)[:, None]
    lasting = (tok_doc == tok_doc[-1]).astype(F32)[:, None]

    def unit_factor(x):
        x = x.astype(F32)
        return jnp.repeat(lax.rsqrt(jnp.sum(x * x, axis=-1) + 1e-06), ratio, axis=1)

    cum = jnp.cumsum(log_decay, axis=0)
    writes = jax.nn.sigmoid(write_logit)
    rq, rk = unit_factor(delta_query), unit_factor(delta_key)
    grown = jnp.exp(cum) * carried
    tail = jnp.exp(cum[-1:] - cum) * writes * lasting
    per = 4
    steps = heads // per
    cols = jnp.stack([cum, rk, rq, grown * rq, tail * rk], axis=-1)
    cols = cols.reshape(toks, steps, per * 5)
    cols = jnp.concatenate([cols, grown.reshape(toks, steps, per)], axis=-1).transpose(1, 0, 2)
    rowv = jnp.stack([cum, writes * rk, grown * rk], axis=-1)
    rowv = rowv.reshape(toks, steps, per * 3).transpose(1, 2, 0)

    delta_out, attended = pl.pallas_call(
        functools.partial(layer_kernel, per, ratio, attn_width ** (-0.5)),
        in_specs=[pl.BlockSpec(memory_space=pltpu.VMEM)] * 11,
        out_specs=[pl.BlockSpec(memory_space=pltpu.VMEM)] * 2,
        out_shape=[
            jax.ShapeDtypeStruct((heads, toks, width), BF16),
            jax.ShapeDtypeStruct((query_heads, toks, attn_width), BF16),
        ],
        scratch_shapes=[
            pltpu.VMEM((SPAN, 2, kv_heads, toks, attn_width), BF16),
            pltpu.VMEM((steps, per, width, width), BF16),
            pltpu.VMEM((steps, per, width, width), F32),
            pltpu.VMEM((steps, per, toks, width), F32),
            pltpu.VMEM((steps, per, toks, width), BF16),
            pltpu.VMEM((SPAN, steps, per, width, width), BF16),
            pltpu.VMEM((SPAN, steps, per, width, width), BF16),
            pltpu.SemaphoreType.DMA((SPAN,)),
            pltpu.SemaphoreType.DMA((SPAN,)),
            pltpu.SemaphoreType.DMA((SPAN, steps)),
            pltpu.SemaphoreType.DMA((SPAN, steps)),
        ],
        compiler_params=pltpu.CompilerParams(
            collective_id=0, has_side_effects=True, vmem_limit_bytes=48 * 1024 * 1024
        ),
        cost_estimate=pl.CostEstimate(flops=8 * 10**9, bytes_accessed=8 * 10**6, transcendentals=2 * 10**6),
        name="layer",
    )(
        heads_first(delta_query),
        heads_first(delta_key),
        heads_first(delta_value),
        cols,
        rowv,
        incl,
        heads_first(output_gate),
        kv,
        heads_first(attn_query),
        mask,
        heads_first(attn_gate),
    )
    return heads_first(delta_out), heads_first(attended)


def solution(mesh):
    tok = P(("groups", "seq"), None, None)
    flat = P(("groups", "seq"), None)
    return jax.shard_map(
        local,
        mesh=mesh,
        in_specs=(tok, tok, tok, flat, flat, tok, tok, tok, tok, tok, P("groups")),
        out_specs=(tok, tok),
        check_vma=False,
    )
```

```python
import functools

import jax
import jax.numpy as jnp
from jax import lax
from jax.experimental import pallas as pl
from jax.experimental.pallas import tpu as pltpu
from jax.sharding import PartitionSpec as P

BLK = 64
SPAN = 4
F32 = jnp.float32
BF16 = jnp.bfloat16
MESH = pl.DeviceIdType.MESH


def mm(a, b):
    return jnp.dot(a, b, preferred_element_type=F32)


def mm_nt(a, b):
    return lax.dot_general(a, b, (((1,), (1,)), ((), ())), preferred_element_type=F32)


def split(x):
    high = x.astype(BF16)
    return high, (x - high.astype(F32)).astype(BF16)


def mm3(a, b):
    ah, al = a
    bh, bl = b
    return mm(ah, bh) + (mm(ah, bl) + mm(al, bh))


def chunk_step(i, heads, ratio, q_ref, k_ref, v_ref, col_ref, row_ref, incl_ref, map_ref, off_ref, base_ref, read_ref, send_ref):
    length = k_ref.shape[1]
    pairs = heads // ratio
    col, row = col_ref[i], row_ref[i]
    incl = incl_ref[...] > 0
    rows = lax.broadcasted_iota(jnp.int32, (length, length), 0)
    cols = lax.broadcasted_iota(jnp.int32, (length, length), 1)
    eye = (rows == cols).astype(F32)
    grams = []
    for j in range(heads // ratio):
        k = k_ref[i * pairs + j]
        grams.append((mm_nt(k, k), mm_nt(q_ref[i * pairs + j], k), k.T))
    decays, lows = [], []
    for h in range(heads):
        c_col, rk_col = col[:, 5 * h : 5 * h + 1], col[:, 5 * h + 1 : 5 * h + 2]
        c_row, bk_row = row[3 * h : 3 * h + 1], row[3 * h + 1 : 3 * h + 2]
        decay = jnp.exp(jnp.where(incl, c_col - c_row, -1e30)) * bk_row
        decays.append(decay)
        lows.append(jnp.where(rows > cols, decay * rk_col * grams[h // ratio][0], 0.0))
    inverses = [eye - jnp.where(rows // 2 == cols // 2, low, 0.0) for low in lows]
    size = 2
    while size < length:
        band = (rows // (2 * size) == cols // (2 * size)) & (rows // size != cols // size)
        parts = [split(x) for x in inverses]
        tops = [mm3(split(jnp.where(band, low, 0.0)), x) for low, x in zip(lows, parts)]
        inverses = [x - mm3(xp, split(t)) for x, xp, t in zip(inverses, parts, tops)]
        size *= 2
    for h in range(heads):
        k_gram, q_gram, k_t = grams[h // ratio]
        k, q, v = k_ref[i * pairs + h // ratio], q_ref[i * pairs + h // ratio], v_ref[i * heads + h]
        rq_col, gq_col, tk_col = (col[:, 5 * h + n : 5 * h + n + 1] for n in (2, 3, 4))
        gain = col[length - 1 : length, 5 * heads + h : 5 * heads + h + 1]
        gk_row = row[3 * h + 2 : 3 * h + 3]
        th, tl = split(inverses[h])
        update = mm(th, v) + mm(tl, v)
        wh, wl = split(inverses[h] * gk_row)
        write = mm(wh, k) + mm(wl, k)
        both = jnp.concatenate([write, update], axis=1)
        th, tl = split(both * tk_col)
        tail = mm(k_t, th) + mm(k_t, tl)
        map_ref[i, h] = (eye * gain - tail[:, :length]).astype(BF16)
        off_ref[i, h] = tail[:, length:]
        send_ref[0, i, h] = tail[:, length:].astype(BF16)
        mix = (decays[h] * rq_col * q_gram).astype(BF16)
        mixed = mm(mix, both.astype(BF16))
        base_ref[i, h] = mixed[:, length:]
        read_ref[i, h] = (gq_col * q.astype(F32) - mixed[:, :length]).astype(BF16)


def layer_kernel(
    per,
    ratio,
    scale,
    q_ref,
    k_ref,
    v_ref,
    col_ref,
    row_ref,
    incl_ref,
    gate_ref,
    kv_ref,
    aq_ref,
    mask_ref,
    agate_ref,
    out_ref,
    att_ref,
    kv_in,
    map_ref,
    off_ref,
    base_ref,
    read_ref,
    send_ref,
    recv_ref,
    kv_send_sem,
    kv_recv_sem,
    send_sem,
    recv_sem,
):
    size = lax.axis_size("seq")
    me = lax.axis_index("seq")
    steps = map_ref.shape[0]

    def device(d):
        return {"seq": lax.rem(me + d + size, size)}

    barrier = pltpu.get_barrier_semaphore()
    for d in range(1, SPAN + 1):
        for side in (d, -d):
            pl.semaphore_signal(barrier, inc=1, device_id=device(side), device_id_type=MESH)
    pl.semaphore_wait(barrier, 2 * SPAN)

    def kv_copy(d):
        return pltpu.make_async_remote_copy(
            src_ref=kv_ref,
            dst_ref=kv_in.at[d - 1],
            send_sem=kv_send_sem.at[d - 1],
            recv_sem=kv_recv_sem.at[d - 1],
            device_id=device(d),
            device_id_type=MESH,
        )

    def hop_copy(hop, i):
        return pltpu.make_async_remote_copy(
            src_ref=send_ref.at[hop, i],
            dst_ref=recv_ref.at[hop, i],
            send_sem=send_sem.at[hop, i],
            recv_sem=recv_sem.at[hop, i],
            device_id=device(1),
            device_id_type=MESH,
        )

    for d in range(1, SPAN + 1):

        @pl.when(me + d < size)
        def _(d=d):
            kv_copy(d).start()

        @pl.when(me < d)
        def _(d=d):
            kv_in[d - 1] = jnp.zeros(kv_in.shape[1:], BF16)

    @pl.when(me == 0)
    def _():
        @pl.loop(0, SPAN * steps)
        def _(r):
            recv_ref[r // steps, r % steps] = jnp.zeros(recv_ref.shape[2:], BF16)

    @pl.loop(0, steps)
    def _(i):
        chunk_step(
            i, per, ratio, q_ref, k_ref, v_ref, col_ref, row_ref, incl_ref, map_ref, off_ref, base_ref, read_ref, send_ref
        )

        @pl.when(me + 1 < size)
        def _():
            hop_copy(0, i).start()

    @pl.loop(0, steps)
    def _(r):
        hop, i = r // steps, r % steps

        @pl.when(me > 0)
        def _():
            hop_copy(hop, i).wait_recv()

        for h in range(per):
            state = mm(map_ref[i, h], recv_ref[hop, i, h]) + off_ref[i, h]
            send_ref[hop + 1, i, h] = state.astype(BF16)

        @pl.when(me + 1 < size)
        def _():
            hop_copy(hop + 1, i).start()

    for d in range(1, SPAN + 1):

        @pl.when(me >= d)
        def _(d=d):
            kv_copy(d).wait_recv()

    group = aq_ref.shape[0] // kv_ref.shape[1]

    @pl.loop(0, kv_ref.shape[1])
    def _(g):
        keys = jnp.concatenate([kv_in[d - 1, 0, g] for d in range(SPAN, 0, -1)] + [kv_ref[0, g]], axis=0)
        values = jnp.concatenate([kv_in[d - 1, 1, g] for d in range(SPAN, 0, -1)] + [kv_ref[1, g]], axis=0)
        for j in range(group):
            scores = mm_nt(aq_ref[g * group + j], keys) * scale + mask_ref[...]
            weights = jnp.exp(scores - jnp.max(scores, axis=-1, keepdims=True))
            total = jnp.sum(weights, axis=-1, keepdims=True)
            mixed = mm(weights.astype(BF16), values)
            gate = agate_ref[g * group + j].astype(F32)
            att_ref[g * group + j] = (mixed / total / (1.0 + jnp.exp(-gate))).astype(BF16)

    @pl.loop(steps, (SPAN - 1) * steps)
    def _(r):
        hop, i = r // steps, r % steps

        @pl.when(me > 0)
        def _():
            hop_copy(hop, i).wait_recv()

        for h in range(per):
            state = mm(map_ref[i, h], recv_ref[hop, i, h]) + off_ref[i, h]
            send_ref[hop + 1, i, h] = state.astype(BF16)

        @pl.when(me + 1 < size)
        def _():
            hop_copy(hop + 1, i).start()

    @pl.loop(0, steps)
    def _(i):

        @pl.when(me > 0)
        def _():
            hop_copy(SPAN - 1, i).wait_recv()

        for h in range(per):
            core = base_ref[i, h] + mm(read_ref[i, h], recv_ref[SPAN - 1, i, h])
            factor = lax.rsqrt(jnp.mean(core * core, axis=-1, keepdims=True) + 1e-06)
            gate = gate_ref[i * per + h].astype(F32)
            out_ref[i * per + h] = (core * factor * (gate / (1.0 + jnp.exp(-gate)))).astype(BF16)

    for d in range(1, SPAN + 1):

        @pl.when(me + d < size)
        def _(d=d):
            kv_copy(d).wait_send()

    @pl.when(me + 1 < size)
    def _():
        @pl.loop(0, SPAN * steps)
        def _(r):
            hop_copy(r // steps, r % steps).wait_send()


def local(
    delta_query,
    delta_key,
    delta_value,
    log_decay,
    write_logit,
    output_gate,
    attn_query,
    attn_key,
    attn_value,
    attn_gate,
    doc_ids,
):
    position = lax.axis_index("seq")
    toks, key_heads, width = delta_key.shape
    heads = delta_value.shape[1]
    ratio = heads // key_heads
    blocks = toks // BLK
    kv_heads, attn_width = attn_key.shape[1:]
    query_heads = attn_query.shape[1]
    group = query_heads // kv_heads
    runs = SPAN + 1

    def heads_first(x):
        return x.transpose(1, 0, 2)

    kv = jnp.stack([heads_first(attn_key), heads_first(attn_value)])

    padded = jnp.concatenate([jnp.full((SPAN * blocks,), -1, doc_ids.dtype), doc_ids])
    window = lax.dynamic_slice_in_dim(padded, position * blocks, runs * blocks)
    key_doc = jnp.repeat(window, BLK)
    tok_doc = key_doc[SPAN * toks :]
    t = jnp.arange(toks, dtype=jnp.int32)
    key_pos = jnp.arange(runs * toks, dtype=jnp.int32) - SPAN * toks
    allowed = (key_doc[None, :] == tok_doc[:, None]) & (key_pos[None, :] <= t[:, None])
    mask = jnp.where(allowed, 0.0, -1e30).astype(F32)
    incl = allowed[:, SPAN * toks :].astype(F32)
    carried = (tok_doc == window[SPAN * blocks - 1]).astype(F32)[:, None]
    lasting = (tok_doc == tok_doc[-1]).astype(F32)[:, None]

    def unit_factor(x):
        x = x.astype(F32)
        return jnp.repeat(lax.rsqrt(jnp.sum(x * x, axis=-1) + 1e-06), ratio, axis=1)

    cum = jnp.cumsum(log_decay, axis=0)
    writes = jax.nn.sigmoid(write_logit)
    rq, rk = unit_factor(delta_query), unit_factor(delta_key)
    grown = jnp.exp(cum) * carried
    tail = jnp.exp(cum[-1:] - cum) * writes * lasting
    per = 4
    steps = heads // per
    cols = jnp.stack([cum, rk, rq, grown * rq, tail * rk], axis=-1)
    cols = cols.reshape(toks, steps, per * 5)
    cols = jnp.concatenate([cols, grown.reshape(toks, steps, per)], axis=-1).transpose(1, 0, 2)
    rowv = jnp.stack([cum, writes * rk, grown * rk], axis=-1)
    rowv = rowv.reshape(toks, steps, per * 3).transpose(1, 2, 0)

    delta_out, attended = pl.pallas_call(
        functools.partial(layer_kernel, per, ratio, attn_width ** (-0.5)),
        in_specs=[pl.BlockSpec(memory_space=pltpu.VMEM)] * 11,
        out_specs=[pl.BlockSpec(memory_space=pltpu.VMEM)] * 2,
        out_shape=[
            jax.ShapeDtypeStruct((heads, toks, width), BF16),
            jax.ShapeDtypeStruct((query_heads, toks, attn_width), BF16),
        ],
        scratch_shapes=[
            pltpu.VMEM((SPAN, 2, kv_heads, toks, attn_width), BF16),
            pltpu.VMEM((steps, per, width, width), BF16),
            pltpu.VMEM((steps, per, width, width), F32),
            pltpu.VMEM((steps, per, toks, width), F32),
            pltpu.VMEM((steps, per, toks, width), BF16),
            pltpu.VMEM((SPAN, steps, per, width, width), BF16),
            pltpu.VMEM((SPAN, steps, per, width, width), BF16),
            pltpu.SemaphoreType.DMA((SPAN,)),
            pltpu.SemaphoreType.DMA((SPAN,)),
            pltpu.SemaphoreType.DMA((SPAN, steps)),
            pltpu.SemaphoreType.DMA((SPAN, steps)),
        ],
        compiler_params=pltpu.CompilerParams(
            collective_id=0, has_side_effects=True, vmem_limit_bytes=48 * 1024 * 1024
        ),
        cost_estimate=pl.CostEstimate(flops=8 * 10**9, bytes_accessed=8 * 10**6, transcendentals=2 * 10**6),
        name="layer",
    )(
        heads_first(delta_query),
        heads_first(delta_key),
        heads_first(delta_value),
        cols,
        rowv,
        incl,
        heads_first(output_gate),
        kv,
        heads_first(attn_query),
        mask,
        heads_first(attn_gate),
    )
    return heads_first(delta_out), heads_first(attended)


def solution(mesh):
    tok = P(("groups", "seq"), None, None)
    flat = P(("groups", "seq"), None)
    return jax.shard_map(
        local,
        mesh=mesh,
        in_specs=(tok, tok, tok, flat, flat, tok, tok, tok, tok, tok, P("groups")),
        out_specs=(tok, tok),
        check_vma=False,
    )
```
